512 devices in a mesh: group: 32 (over x_lo, z), rep: 8 (over y, core), tp: 2 (over x_hi).
Axes of the slice: x: 4 (x_hi: 2, x_lo: 2; x = x_hi * 2 + x_lo), y: 4, z: 16, core: 2. Of those that a mesh axis runs over, the one named last changes fastest.
Arguments:
- prompt_states: bfloat16 [4096, 4, 8192], P('group', None, 'rep'), may hold values from -6 to 6
- kv_weight: bfloat16 [8192, 2, 1024], P('rep', None, 'tp'), may hold values from -0.0625 to 0.0625
- queries: bfloat16 [1024, 8, 8192], P(('group', 'rep'), None, 'tp'), may hold values from -600 to 600
- new_kv: bfloat16 [1024, 8, 2, 1024], P(('group', 'rep'), None, None, 'tp'), may hold values from -6 to 6
- prompt_pages: int32 [4], replicated, may hold values from 16 to 32, as said below
- decoder_prompt: int32 [32], replicated, may hold values from 0 to 3, as said below
- sample_count: int32 [32], P('group'), may hold values from 1 to 32, as said below
Outputs:
- attention_out: bfloat16 [1024, 8, 8192], P(('group', 'rep'), None, 'tp')
The draws below stay inside these ranges and needn't reach their ends.
Inputs may be any that keep to these rules, and one draw needn't show every extreme that they name: `prompt_pages`: some prompt has all 32 pages. `decoder_prompt`: each prompt is sampled by exactly 32 // 4 decode groups. `sample_count`: some group has all its sample rows live.
All inputs are finite; a program needn't handle non-finite values.
Results may differ from the reference program's by a relative error of at most 0.013.
Values may be sent and summed in bfloat16 or wider, within the bound.
A program may use at most 64 MiB of HBM per device.

```python
import jax
import jax.numpy as jnp
from jax import lax

D = 8192
QH = 64
KVH = 8
HD = 128
PAGE = 128
STEPS = 8
PROMPTS = 4
S_DEV = 4
L = 4096
SAMPLES = 1024
N_GROUP = 32
N_REP = 8


def shared_keys(key):
    return jnp.clip(jax.random.normal(key, (SAMPLES, STEPS, KVH, HD), jnp.float32), -6.0, 6.0)


def draw_queries(key, part):
    aligned = shared_keys(key)
    key = jax.random.fold_in(key, 11)
    noise_key = jax.random.fold_in(key, 0)
    row_shape = (SAMPLES, STEPS, KVH, QH // KVH)
    noise_rows = 2.4 * jax.random.normal(noise_key, row_shape + (HD,), jnp.float32)
    query_rows = 0.75 * aligned[:, :, :, None, :] + noise_rows
    query_rows = jnp.clip(query_rows, -600.0, 600.0)
    return query_rows.reshape(SAMPLES, STEPS, QH * HD).astype(jnp.bfloat16)


def draw_new_kv(key, part):
    aligned = shared_keys(key)
    key = jax.random.fold_in(key, 12)
    value_rows = jnp.clip(jax.random.normal(key, (SAMPLES, STEPS, KVH, HD), jnp.float32), -6.0, 6.0)
    stacked = jnp.stack([aligned, value_rows], axis=2)
    return stacked.reshape(SAMPLES, STEPS, 2, KVH * HD).astype(jnp.bfloat16)


def draw_prompt_pages(key, part):
    key = jax.random.fold_in(key, 21)
    first_key, second_key = jax.random.split(key)
    most_pages = L // PAGE
    page_counts = jax.random.randint(first_key, (PROMPTS,), most_pages // 2, most_pages + 1)
    longest = jax.random.randint(second_key, (), 0, PROMPTS)
    return jnp.where(jnp.arange(PROMPTS) == longest, most_pages, page_counts).astype(jnp.int32)


def draw_decoder_prompt(key, part):
    key = jax.random.fold_in(key, 22)
    balanced = jnp.arange(N_GROUP, dtype=jnp.int32) % PROMPTS
    return jax.random.permutation(key, balanced).astype(jnp.int32)


def draw_sample_count(key, part):
    key = jax.random.fold_in(key, 23)
    first_key, second_key = jax.random.split(key)
    most_rows = S_DEV * N_REP
    counts = jax.random.randint(first_key, (N_GROUP,), 1, most_rows + 1)
    fullest = jax.random.randint(second_key, (), 0, N_GROUP)
    return jnp.where(jnp.arange(N_GROUP) == fullest, most_rows, counts).astype(jnp.int32)


def block_scale(own_key, dims, shards, smallest, largest):
    level, own = 1.0, jax.random.fold_in(own_key, 6)
    for dim, blocks in shards:
        draws = jnp.exp(jax.random.uniform(jax.random.fold_in(own, dim), (blocks,), jnp.float32, smallest / len(shards), largest / len(shards)))
        level = level * jnp.repeat(draws, dims[dim] // blocks).reshape([-1 if axis == dim else 1 for axis in range(len(dims))])
    return level


def bell_draw(stream_key, extent, scale, limit, pieces=(), kind=jnp.bfloat16):
    factor_of = block_scale(stream_key, extent, pieces, -0.22, 0.18) if pieces else 1.0
    drawn = jax.random.normal(stream_key, extent, jnp.float32) * scale * factor_of
    return jnp.minimum(jnp.maximum(drawn, -limit), limit).astype(kind)


def setup_inputs(seed: int = 0) -> dict:
    streams_of = jax.random.split(jax.random.key(seed), 8)
    prompt_states = bell_draw(streams_of[0], (L, PROMPTS, D), 1.0, 6.0, ((0, 32), (2, 8)))
    kv_weight = bell_draw(streams_of[1], (D, 2, KVH * HD), D ** -0.5, 0.0625, ((0, 8), (2, 2)))
    queries = draw_queries(jax.random.fold_in(streams_of[7], 71), 0)
    new_kv = draw_new_kv(jax.random.fold_in(streams_of[7], 71), 0)
    prompt_pages = draw_prompt_pages(jax.random.fold_in(streams_of[7], 71), 0)
    decoder_prompt = draw_decoder_prompt(jax.random.fold_in(streams_of[7], 71), 0)
    sample_count = draw_sample_count(jax.random.fold_in(streams_of[7], 71), 0)
    return {"prompt_states": prompt_states, "kv_weight": kv_weight, "queries": queries, "new_kv": new_kv, "prompt_pages": prompt_pages, "decoder_prompt": decoder_prompt, "sample_count": sample_count}


def reference(prompt_states, kv_weight, queries, new_kv, prompt_pages, decoder_prompt, sample_count):
    factor = HD ** -0.5
    query_group = QH // KVH
    rows_group = N_REP * S_DEV
    partial_value = jnp.dot(prompt_states.reshape(L * PROMPTS, D), kv_weight.reshape(D, 2 * KVH * HD), preferred_element_type=jnp.float32)
    kv_cache = partial_value.astype(jnp.bfloat16).reshape(L, PROMPTS, 2, KVH, HD)
    query_all = queries.reshape(N_GROUP, rows_group, STEPS, KVH, query_group, HD)
    new_all = new_kv.reshape(N_GROUP, rows_group, STEPS, 2, KVH, HD)
    positions = jnp.arange(L, dtype=jnp.int32)
    causal = jnp.arange(STEPS, dtype=jnp.int32)[:, None] >= jnp.arange(STEPS, dtype=jnp.int32)[None, :]
    row_ids = jnp.arange(rows_group, dtype=jnp.int32)
    replica_ids = row_ids // S_DEV
    slot_ids = row_ids % S_DEV

    def one_group(group_index):
        own_prompt = decoder_prompt[group_index].astype(jnp.int32)
        prompt_kv = lax.dynamic_index_in_dim(kv_cache, own_prompt, 1, keepdims=False)
        key_live = positions < prompt_pages[own_prompt] * PAGE
        query_block = lax.dynamic_index_in_dim(query_all, group_index, 0, keepdims=False)
        new_block = lax.dynamic_index_in_dim(new_all, group_index, 0, keepdims=False)

        def one_head(head_index):
            query_head = lax.dynamic_index_in_dim(query_block, head_index, 2, keepdims=False).astype(jnp.float32)
            prompt_keys = lax.dynamic_index_in_dim(prompt_kv[:, 0], head_index, 1, keepdims=False).astype(jnp.float32)
            prompt_values = lax.dynamic_index_in_dim(prompt_kv[:, 1], head_index, 1, keepdims=False).astype(jnp.float32)
            new_keys = lax.dynamic_index_in_dim(new_block[:, :, 0], head_index, 2, keepdims=False).astype(jnp.float32)
            new_values = lax.dynamic_index_in_dim(new_block[:, :, 1], head_index, 2, keepdims=False).astype(jnp.float32)
            scores = jnp.einsum('sagd,nd->sagn', query_head, prompt_keys) * factor
            new_scores = jnp.einsum('sagd,sbd->sagb', query_head, new_keys) * factor
            new_mask = causal[None, :, None, :]
            row_max = jnp.maximum(jnp.max(jnp.where(key_live, scores, -jnp.inf), axis=-1),
                                  jnp.max(jnp.where(new_mask, new_scores, -jnp.inf), axis=-1))
            weights = jnp.where(key_live, jnp.exp(scores - row_max[..., None]), 0.0)
            new_weights = jnp.where(new_mask, jnp.exp(new_scores - row_max[..., None]), 0.0)
            weight_sum = jnp.sum(weights, axis=-1) + jnp.sum(new_weights, axis=-1)
            rounded = lax.optimization_barrier(weights.astype(jnp.bfloat16)).astype(jnp.float32)
            new_rounded = lax.optimization_barrier(new_weights.astype(jnp.bfloat16)).astype(jnp.float32)
            mixed = jnp.einsum('sagn,nd->sagd', rounded, prompt_values) + jnp.einsum('sagb,sbd->sagd', new_rounded, new_values)
            return mixed / weight_sum[..., None]

        heads_out = lax.map(one_head, jnp.arange(KVH, dtype=jnp.int32))
        heads_out = jnp.transpose(heads_out, (1, 2, 0, 3, 4))
        row_live = slot_ids * N_REP + replica_ids < sample_count[group_index]
        return jnp.where(row_live[:, None, None, None, None], heads_out, 0.0)

    every_group = lax.map(one_group, jnp.arange(N_GROUP, dtype=jnp.int32))
    return every_group.reshape(SAMPLES, STEPS, QH * HD).astype(jnp.bfloat16)
```

```python
import functools

import jax
import jax.numpy as jnp
from jax import lax
from jax.experimental import pallas as pl
from jax.experimental.pallas import tpu as pltpu
from jax.sharding import PartitionSpec as P

MESH = pl.DeviceIdType.MESH
F32 = jnp.float32
BF16 = jnp.bfloat16

HD = 128
PAGE = 128
QG = 8
STEPS = 8
S_DEV = 4
NX = 2
NY = 4
PROMPTS = 4
CHUNKS = 4
TOK = PAGE // CHUNKS
ROWS = TOK * PROMPTS
HALF = ROWS // 2
QROWS = QG * S_DEV * STEPS
SCALE = HD**-0.5 * 1.4426950408889634


def kernel(
    nz,
    x_hbm,
    w_hbm,
    q_hbm,
    n_hbm,
    pages_ref,
    dec_ref,
    cnt_ref,
    o_hbm,
    xv,
    wv,
    nv,
    wr,
    part,
    pair,
    ra,
    sb,
    rb,
    fin,
    unit,
    land,
    picked,
    kv,
    qrec,
    nstage,
    nrec,
    qs,
    acc,
    mx,
    ostage,
    in_sem,
    pair_s,
    pair_r,
    ra_s,
    ra_r,
    rb_s,
    rb_r,
    z_s,
    z_r,
    x_s,
    x_r,
    c_s,
    c_r,
    f_s,
    f_r,
    q_s,
    q_r,
    n_s,
    n_r,
    o_s,
    o_r,
    l_s,
):
    last = nz // 2
    g = lax.axis_index("group")
    r = lax.axis_index("rep")
    cx = g // nz
    z = g % nz
    y = r // 2
    k = r % 2
    turn = 1 - 2 * k
    to_a = {"group": cx * nz + (z + turn + nz) % nz}
    to_b = {"group": cx * nz + (z - turn + nz) % nz}
    to_x = {"group": (1 - cx) * nz + z}
    to_core = {"rep": y * 2 + 1 - k}
    y_opp, y_up, y_dn = (y + 2) % NY, (y + 1) % NY, (y + 3) % NY
    to_opp = {"rep": y_opp * 2 + k}
    to_up = {"rep": y_up * 2 + k}
    to_dn = {"rep": y_dn * 2 + k}

    def remote(src, dst, ss, rs, to):
        return pltpu.make_async_remote_copy(
            src_ref=src, dst_ref=dst, send_sem=ss, recv_sem=rs, device_id=to, device_id_type=MESH
        )

    get_w = pltpu.make_async_copy(w_hbm, wv, in_sem.at[0])
    get_x = pltpu.make_async_copy(x_hbm, xv, in_sem.at[1])
    get_n = pltpu.make_async_copy(n_hbm, nv, in_sem.at[2])
    get_w.start()
    get_x.start()
    get_n.start()

    everyone = (to_a, to_b, to_x, to_core, to_opp, to_up, to_dn)
    barrier = pltpu.get_barrier_semaphore()
    for other in everyone:
        pl.semaphore_signal(barrier, inc=1, device_id=other, device_id_type=MESH)
    pl.semaphore_wait(barrier, len(everyone))

    def pair_copy(j):
        return remote(part.at[j, 1 - k], pair.at[j], pair_s.at[j], pair_r.at[j], to_core)

    def ra_copies(j):
        h0, h1 = pl.ds(0, HALF), pl.ds(HALF, HALF)
        plan = (
            (y_opp, h0, 0, to_up),
            (y_up, h1, 1, to_up),
            (y_opp, h1, 2, to_dn),
            (y_dn, h0, 3, to_dn),
        )
        return [
            remote(part.at[j, k, head, rows], ra.at[j, i], ra_s.at[j, i], ra_r.at[j, i], to)
            for head, rows, i, to in plan
        ]

    def rb_copies(j):
        return [
            remote(sb.at[j, i], rb.at[j, i], rb_s.at[j, i], rb_r.at[j, i], to)
            for i, to in ((0, to_up), (1, to_dn))
        ]

    def z_copy(way, s, j):
        src = unit.at[j] if isinstance(s, int) and s == 1 else land.at[way, s - 2, j]
        return remote(
            src, land.at[way, s - 1, j], z_s.at[way, s - 1, j], z_r.at[way, s - 1, j],
            to_a if way == 0 else to_b,
        )

    def z_arrival(way, s, j):
        return remote(
            unit.at[j], land.at[way, s - 1, j], z_s.at[way, s - 1, j], z_r.at[way, s - 1, j],
            to_a if way == 0 else to_b,
        )

    def x_copy(s, n):
        return remote(
            picked.at[s, pl.ds(0, n)], kv.at[k, s, cx, pl.ds(0, n)], x_s.at[s], x_r.at[s], to_x
        )

    def own_copy(s, n):
        here = kv.at[k, s, cx, pl.ds(0, n)]
        return remote(here, here, c_s.at[s], c_r.at[s], to_core)

    def fwd_copy(s, n):
        here = kv.at[k, s, 1 - cx, pl.ds(0, n)]
        return remote(here, here, f_s.at[s], f_r.at[s], to_core)

    def x_arrival(s, n):
        return remote(
            picked.at[s, pl.ds(0, n)], kv.at[k, s, 1 - cx, pl.ds(0, n)], x_s.at[s], x_r.at[s], to_x
        )

    def own_arrival(s, n):
        there = kv.at[1 - k, s, cx, pl.ds(0, n)]
        return remote(there, there, c_s.at[s], c_r.at[s], to_core)

    def fwd_arrival(s, n):
        there = kv.at[1 - k, s, 1 - cx, pl.ds(0, n)]
        return remote(there, there, f_s.at[s], f_r.at[s], to_core)

    ways = ((y_opp, to_opp, 0), (y_up, to_up, 2), (y_dn, to_dn, 1))

    def q_copies():
        return [
            remote(
                q_hbm.at[:, pl.ds(pl.multiple_of(yy * QG * HD, QG * HD), QG * HD)],
                qrec.at[slot], q_s.at[i], q_r.at[slot], to,
            )
            for i, (yy, to, slot) in enumerate(ways)
        ]

    def n_copies():
        return [
            remote(nstage.at[yy], nrec.at[slot], n_s.at[i], n_r.at[slot], to)
            for i, (yy, to, slot) in enumerate(ways)
        ]

    my_columns = pl.ds(pl.multiple_of(y * QG * HD, QG * HD), QG * HD)
    q_own = pltpu.make_async_copy(q_hbm.at[:, my_columns], qrec.at[3], l_s.at[0])
    n_own = pltpu.make_async_copy(nstage.at[y], nrec.at[3], l_s.at[1])
    o_own = pltpu.make_async_copy(ostage.at[3], o_hbm.at[:, my_columns], l_s.at[2])

    mine = dec_ref[g]
    theirs = dec_ref[(1 - cx) * nz + z]
    limit = pages_ref[mine]
    count = cnt_ref[0]

    def choose(blocks, which):
        out = blocks[3]
        for p in (2, 1, 0):
            out = jnp.where(which == p, blocks[p], out)
        return out

    def pick(blocks, s, pos, j):
        rows = pl.ds(j * TOK, TOK)
        kv[k, s, cx, pos, rows, :] = choose(blocks, mine)
        picked[s, pos, rows, :] = choose(blocks, theirs)

    def project(j):
        rows = xv[pl.ds(j * TOK, TOK)].reshape(ROWS, xv.shape[2])
        got = jnp.dot(rows, wr[...], preferred_element_type=F32)
        for kind in range(2):
            for h in range(NY):
                first = (kind * NY + h) * HD
                part[j, kind, h] = got[:, first : first + HD]
        pair_copy(j).start()

    def sum_pair(j):
        pair_copy(j).wait_recv()
        for h in range(NY):
            part[j, k, h] = part[j, k, h] + pair[j, h]
        for copy in ra_copies(j):
            copy.start()

    def sum_next(j):
        for copy in ra_copies(j):
            copy.wait_recv()
        sb[j, 0] = part[j, k, y_up, pl.ds(0, HALF), :] + ra[j, 0]
        sb[j, 1] = part[j, k, y_dn, pl.ds(HALF, HALF), :] + ra[j, 2]
        for copy in rb_copies(j):
            copy.start()

    def sum_last(j):
        for copy in rb_copies(j):
            copy.wait_recv()
        fin[j, pl.ds(0, HALF), :] = part[j, k, y, pl.ds(0, HALF), :] + ra[j, 3] + rb[j, 0]
        fin[j, pl.ds(HALF, HALF), :] = part[j, k, y, pl.ds(HALF, HALF), :] + ra[j, 1] + rb[j, 1]
        blocks = []
        for p in range(PROMPTS):
            block = fin[j, pl.ds(p, TOK, stride=PROMPTS), :].astype(BF16)
            unit[j, p] = block
            blocks.append(block)
        z_copy(0, 1, j).start()
        z_copy(1, 1, j).start()
        pick(blocks, 0, 0, j)

    get_w.wait()
    wr[...] = wv[...].reshape(wr.shape)
    get_x.wait()
    for t in range(CHUNKS + 3):
        if t < CHUNKS:
            project(t)
        if 0 <= t - 1 < CHUNKS:
            sum_pair(t - 1)
        if 0 <= t - 2 < CHUNKS:
            sum_next(t - 2)
        if 0 <= t - 3 < CHUNKS:
            sum_last(t - 3)
        if t == 0:
            get_n.wait()
            flat = nv[...].reshape(S_DEV * STEPS, nv.shape[2] * nv.shape[3])
            for h in range(NY):
                for kind in range(2):
                    first = (kind * NY + h) * HD
                    nstage[h, kind] = flat[:, first : first + HD]
            q_own.start()
            n_own.start()
        if t == CHUNKS:
            for copy in q_copies() + n_copies():
                copy.start()
    x_copy(0, 1).start()
    own_copy(0, 1).start()

    def begin(i):
        for h in range(QG):
            qs[i, pl.ds(h * S_DEV * STEPS, S_DEV * STEPS), :] = qrec[i, :, pl.ds(h * HD, HD)]
        keys, values = nrec[i, 0], nrec[i, 1]
        scores = lax.dot_general(
            qs[i], keys, (((1,), (1,)), ((), ())), preferred_element_type=F32
        )
        row = lax.broadcasted_iota(jnp.int32, scores.shape, 0)
        col = lax.broadcasted_iota(jnp.int32, scores.shape, 1)
        row_step, col_step = row % STEPS, col % STEPS
        same = (row // STEPS) % S_DEV == col // STEPS
        scores = jnp.where(same & (col_step <= row_step), scores, -jnp.inf)
        top = jnp.max(scores, axis=1, keepdims=True)
        weights = jnp.exp2((scores - top) * SCALE)
        wide = jnp.concatenate([values, jnp.ones_like(values)], axis=1)
        acc[i] = jnp.dot(weights.astype(BF16), wide, preferred_element_type=F32)
        mx[i] = jnp.broadcast_to(top, (QROWS, HD))

    def attend(s, i, both):
        if both:
            keys = kv[0, s].reshape(4 * PAGE, HD)
            values = jnp.concatenate([kv[1, s, c, pos] for c in range(2) for pos in (1, 0)], axis=0)
            sources = ((z - s + nz) % nz, (z + s) % nz)
        else:
            keys = jnp.concatenate([kv[0, s, c, 0] for c in range(2)], axis=0)
            values = jnp.concatenate([kv[1, s, c, 0] for c in range(2)], axis=0)
            sources = ((z + s) % nz,)
        scores = lax.dot_general(
            qs[i], keys, (((1,), (1,)), ((), ())), preferred_element_type=F32
        )
        width = len(sources) * PAGE
        pieces = [scores[:, :width]]
        for n, source in enumerate(sources):
            piece = scores[:, width + n * PAGE : width + (n + 1) * PAGE]
            pieces.append(jnp.where(nz + source < limit, piece, -jnp.inf))
        scores = jnp.concatenate(pieces, axis=1)
        before = mx[i][:, :1]
        top = jnp.maximum(before, jnp.max(scores, axis=1, keepdims=True))
        shrink = jnp.exp2((before - top) * SCALE)
        weights = jnp.exp2((scores - top) * SCALE)
        wide = jnp.concatenate([values, jnp.ones_like(values)], axis=1)
        acc[i] = acc[i] * shrink + jnp.dot(weights.astype(BF16), wide, preferred_element_type=F32)
        mx[i] = jnp.broadcast_to(top, (QROWS, HD))

    def ready(s, n):
        own_arrival(s, n).wait_recv()
        fwd_arrival(s, n).wait_recv()

    def pass_on(s, n):
        x_arrival(s, n).wait_recv()
        fwd_copy(s, n).start()

    def hop(s, j):
        z_arrival(0, s, j).wait_recv()
        z_copy(0, s + 1, j).start()
        z_arrival(1, s, j).wait_recv()

        @pl.when(s < last - 1)
        def _():
            z_copy(1, s + 1, j).start()

        for way in range(2):
            pick([land[way, s - 1, j, p] for p in range(PROMPTS)], s, way, j)

    def hop_done(s):
        x_copy(s, 2).start()
        own_copy(s, 2).start()

    q_own.wait()
    n_own.wait()
    for copy in q_copies() + n_copies():
        copy.wait_recv()

    def first_step(j, carry):
        hop(1, j)
        begin(j)
        return carry

    lax.fori_loop(0, CHUNKS, first_step, 0)
    pass_on(0, 1)
    hop_done(1)

    ready(0, 1)

    def second_step(j, carry):
        hop(2, j)
        attend(0, j, False)
        return carry

    lax.fori_loop(0, CHUNKS, second_step, 0)
    pass_on(1, 2)
    hop_done(2)

    def later_step(s, carry):
        ready(s - 2, 2)

        def inner(j, c):
            hop(s, j)
            attend(s - 2, j, True)
            return c

        lax.fori_loop(0, CHUNKS, inner, 0)
        pass_on(s - 1, 2)
        hop_done(s)
        return carry

    lax.fori_loop(3, last, later_step, 0)

    ready(last - 2, 2)

    def last_step(j, carry):
        z_arrival(0, last, j).wait_recv()
        pick([land[0, last - 1, j, p] for p in range(PROMPTS)], last, 0, j)
        attend(last - 2, j, True)
        return carry

    lax.fori_loop(0, CHUNKS, last_step, 0)
    x_copy(last, 1).start()
    own_copy(last, 1).start()
    pass_on(last - 1, 2)
    pass_on(last, 1)
    ready(last - 1, 2)

    def tail_step(j, carry):
        attend(last - 1, j, True)
        return carry

    lax.fori_loop(0, CHUNKS, tail_step, 0)
    ready(last, 1)

    def o_copy(i, to):
        return remote(ostage.at[i], o_hbm.at[:, my_columns], o_s.at[i], o_r.at[i], to)

    for i, (yy, to) in enumerate(((y_opp, to_opp), (y_up, to_up), (y_dn, to_dn), (y, None))):
        attend(last, i, False)
        result = acc[i][:, :HD] / acc[i][:, HD:]
        rows = S_DEV * STEPS
        result = jnp.concatenate([result[h * rows : (h + 1) * rows] for h in range(QG)], axis=1)
        sample = lax.broadcasted_iota(jnp.int32, result.shape, 0) // STEPS
        live = sample * (NY * 2) + (yy * 2 + k) < count
        ostage[i] = jnp.where(live, result, 0.0).astype(BF16)
        if to is None:
            o_own.start()
        else:
            o_copy(i, to).start()

    for j in range(CHUNKS):
        pair_copy(j).wait_send()
        for copy in ra_copies(j) + rb_copies(j):
            copy.wait_send()

    def sent(s, carry):
        for j in range(CHUNKS):
            z_arrival(0, s, j).wait_send()

            @pl.when(s < last)
            def _():
                z_arrival(1, s, j).wait_send()

        return carry

    lax.fori_loop(1, last + 1, sent, 0)
    for s, n in ((0, 1), (last, 1)):
        x_copy(s, n).wait_send()
        own_copy(s, n).wait_send()
        fwd_copy(s, n).wait_send()

    def sent_two(s, carry):
        x_copy(s, 2).wait_send()
        own_copy(s, 2).wait_send()
        fwd_copy(s, 2).wait_send()
        return carry

    lax.fori_loop(1, last, sent_two, 0)
    for copy in q_copies() + n_copies():
        copy.wait_send()
    o_own.wait()
    for i, (yy, to) in enumerate(((y_opp, to_opp), (y_up, to_up), (y_dn, to_dn))):
        o_copy(i, to).wait_send()
        yyy = (y_opp, y_dn, y_up)[i]
        there = o_hbm.at[:, pl.ds(pl.multiple_of(yyy * QG * HD, QG * HD), QG * HD)]
        remote(ostage.at[i], there, o_s.at[i], o_r.at[i], to).wait_recv()


def body(nz, prompt_states, kv_weight, queries, new_kv, prompt_pages, decoder_prompt, sample_count):
    steps = nz // 2
    depth, width = kv_weight.shape[0], 2 * kv_weight.shape[2]
    any_space = pl.BlockSpec(memory_space=pl.ANY)
    smem = pl.BlockSpec(memory_space=pltpu.SMEM)
    rows = S_DEV * STEPS
    dma = pltpu.SemaphoreType.DMA
    out = pl.pallas_call(
        functools.partial(kernel, nz),
        out_shape=jax.ShapeDtypeStruct((rows, queries.shape[2]), BF16),
        in_specs=[any_space] * 4 + [smem] * 3,
        out_specs=any_space,
        scratch_shapes=[
            pltpu.VMEM(prompt_states.shape, BF16),
            pltpu.VMEM(kv_weight.shape, BF16),
            pltpu.VMEM(new_kv.shape, BF16),
            pltpu.VMEM((depth, width), BF16),
            pltpu.VMEM((CHUNKS, 2, NY, ROWS, HD), F32),
            pltpu.VMEM((CHUNKS, NY, ROWS, HD), F32),
            pltpu.VMEM((CHUNKS, 4, HALF, HD), F32),
            pltpu.VMEM((CHUNKS, 2, HALF, HD), F32),
            pltpu.VMEM((CHUNKS, 2, HALF, HD), F32),
            pltpu.VMEM((CHUNKS, ROWS, HD), F32),
            pltpu.VMEM((CHUNKS, PROMPTS, TOK, HD), BF16),
            pltpu.VMEM((2, steps, CHUNKS, PROMPTS, TOK, HD), BF16),
            pltpu.VMEM((steps + 1, 2, PAGE, HD), BF16),
            pltpu.VMEM((2, steps + 1, NX, 2, PAGE, HD), BF16),
            pltpu.VMEM((NY, rows, QG * HD), BF16),
            pltpu.VMEM((NY, 2, rows, HD), BF16),
            pltpu.VMEM((NY, 2, rows, HD), BF16),
            pltpu.VMEM((NY, QROWS, HD), BF16),
            pltpu.VMEM((NY, QROWS, 2 * HD), F32),
            pltpu.VMEM((NY, QROWS, HD), F32),
            pltpu.VMEM((NY, rows, QG * HD), BF16),
            dma((3,)),
            dma((CHUNKS,)),
            dma((CHUNKS,)),
            dma((CHUNKS, 4)),
            dma((CHUNKS, 4)),
            dma((CHUNKS, 2)),
            dma((CHUNKS, 2)),
            dma((2, steps, CHUNKS)),
            dma((2, steps, CHUNKS)),
            dma((steps + 1,)),
            dma((steps + 1,)),
            dma((steps + 1,)),
            dma((steps + 1,)),
            dma((steps + 1,)),
            dma((steps + 1,)),
            dma((3,)),
            dma((3,)),
            dma((3,)),
            dma((3,)),
            dma((3,)),
            dma((3,)),
            dma((3,)),
        ],
        compiler_params=pltpu.CompilerParams(
            collective_id=0, has_side_effects=True, vmem_limit_bytes=48 * 2**20
        ),
        cost_estimate=pl.CostEstimate(
            flops=6_500_000_000, bytes_accessed=4_000_000, transcendentals=4_200_000
        ),
    )(
        prompt_states,
        kv_weight,
        queries.reshape(rows, queries.shape[2]),
        new_kv,
        prompt_pages,
        decoder_prompt,
        sample_count,
    )
    return out.reshape(queries.shape)


def solution(mesh):
    placed = (
        P("group", None, "rep"),
        P("rep", None, "tp"),
        P(("group", "rep"), None, "tp"),
        P(("group", "rep"), None, None, "tp"),
        P(),
        P(),
        P("group"),
    )
    return jax.shard_map(
        functools.partial(body, mesh.shape["group"] // NX),
        mesh=mesh,
        in_specs=placed,
        out_specs=P(("group", "rep"), None, "tp"),
        check_vma=False,
    )
```
